32 devices in a mesh: row: 8 (over y, x, core), col: 4 (over z).
Axes of the slice: x: 2, y: 2, z: 4, core: 2. Of those that a mesh axis runs over, the one named last changes fastest.
Arguments:
- coeffs: bfloat16 [16384, 1024], P('row', 'col'), may hold values from -6 to 6
- intersection: bfloat16 [16384, 16384], P('row', 'col'), may hold values from -0.006225586 to 0.006225586
- coeff_mask: int32 [128, 8], P('row', 'col'), may hold values 0 or 1
- intersection_mask: int32 [128, 128], P('row', 'col'), may hold values 0 or 1
Outputs:
- gradient: float32 [1024, 1024], P('row', 'col')
The draws below stay inside these ranges and needn't reach their ends.
All inputs are finite; a program needn't handle non-finite values. No bound on the sum of `coeff_mask` or of `intersection_mask` on one device may be relied on, other than what follows from the above.
Results may differ from the reference program's by a relative error of at most 0.0029.
Values may be sent and summed in bfloat16 or wider, within the bound.
A program may use at most 128 MiB of HBM per device.

```python
import jax
import jax.numpy as jnp
from jax import lax

BLK = 128
ORB_BLOCKS = 8
ORDER = 16384
ORBITALS = 1024
N_ROW = 8
N_COL = 4


def touch_ends(drawn, key, low, largest):
    longest = drawn.shape.index(max(drawn.shape))
    spots = []
    for shift in (0, 1):
        where = [jax.random.randint(jax.random.fold_in(key, axis), (), 0, length) for axis, length in enumerate(drawn.shape)]
        where[longest] = (where[longest] + shift) % drawn.shape[longest]
        spots.append(tuple(where))
    return drawn.at[spots[0]].set(low).at[spots[1]].set(largest)


def shard_levels(own_key, dims, cuts, smallest, high):
    def one(position, parts):
        steps = jax.random.uniform(jax.random.fold_in(jax.random.fold_in(own_key, 6), position), (parts,), jnp.float32, smallest / len(cuts), high / len(cuts))
        return jnp.repeat(jnp.exp(steps), dims[position] // parts).reshape((-1,) + (1,) * (len(dims) - position - 1))

    level = one(*cuts[0])
    for cut in cuts[1:]:
        level = level * one(*cut)
    return level


def bell_draw(rng, extent, scale, bound, cuts=(), kind=jnp.bfloat16):
    loudness = shard_levels(rng, extent, cuts, -0.22, 0.18) if cuts else 1.0
    drawn = jax.random.normal(rng, extent, jnp.float32) * scale * loudness
    return jnp.minimum(jnp.maximum(drawn, -bound), bound).astype(kind)


def setup_inputs(seed: int = 0) -> dict:
    seeds = jax.random.split(jax.random.key(seed), 5)
    coeffs = bell_draw(seeds[0], (ORDER, ORBITALS), 1.0, 6.0, ((0, 8), (1, 4)))
    intersection = bell_draw(seeds[1], (ORDER, ORDER), 0.0009765625, 0.006225586, ((0, 8), (1, 4)))
    coeff_mask = touch_ends((jax.random.randint(seeds[2], (ORDER // BLK, ORB_BLOCKS), 0, 5) < 2).astype(jnp.int32), jax.random.fold_in(seeds[2], 1), 0, 1)
    intersection_mask = touch_ends((jax.random.randint(seeds[3], (ORDER // BLK, ORDER // BLK), 0, 5) < 2).astype(jnp.int32), jax.random.fold_in(seeds[3], 1), 0, 1)
    return {"coeffs": coeffs, "intersection": intersection, "coeff_mask": coeff_mask, "intersection_mask": intersection_mask}


def mask_blocks(data, mask):
    rows, cols = data.shape
    shaped = data.reshape(rows // BLK, BLK, cols // BLK, BLK)
    return (shaped * mask.astype(data.dtype)[:, None, :, None]).reshape(rows, cols)


def reference(coeffs, intersection, coeff_mask, intersection_mask):
    masked_c = mask_blocks(coeffs, coeff_mask).astype(jnp.float32)
    band = ORDER // N_ROW
    width = ORDER // N_COL
    slabs = intersection.reshape(N_ROW, band, ORDER)
    slab_masks = intersection_mask.reshape(N_ROW, band // BLK, ORDER // BLK)
    c_slabs = masked_c.reshape(N_ROW, band, ORBITALS)

    def accumulate(total, item):
        slab, slab_mask, c_rows = item
        masked_s = mask_blocks(slab, slab_mask).astype(jnp.float32)

        def group(inner, index):
            first = (index * width).astype(jnp.int32)
            s_part = lax.dynamic_slice_in_dim(masked_s, first, width, 1)
            c_part = lax.dynamic_slice_in_dim(masked_c, first, width, 0)
            partial_value = jnp.dot(s_part, c_part, precision=lax.Precision.HIGHEST).astype(jnp.bfloat16)
            partial_value = lax.optimization_barrier(partial_value).astype(jnp.float32)
            inner = inner + jnp.dot(c_rows.T, partial_value, precision=lax.Precision.HIGHEST)
            return inner, None

        total, unused = lax.scan(group, total, jnp.arange(N_COL, dtype=jnp.int32))
        return total, None

    start = jnp.zeros((ORBITALS, ORBITALS), jnp.float32)
    gradient, unused = lax.scan(accumulate, start, (slabs, slab_masks, c_slabs))
    return gradient
```

```python
import functools

import jax
import jax.numpy as jnp
from jax import lax
from jax.experimental import pallas as pl
from jax.experimental.pallas import tpu as pltpu
from jax.sharding import PartitionSpec as P

BLK = 128
CHUNKS = 4
BF = jnp.bfloat16
F32 = jnp.float32


def kernel(
    rn, zn, cmask, smask, c_ref, s_hbm, out_ref,
    s_buf, rows, rows_t, cols, prod, g_own, g_sib, g_got, x_out, x_in, z_out, z_in,
    s_sem, up_send, dn_send, z_recv, ring_send, ring_recv, sib_send, sib_recv, loc_sem,
    gs_send, gs_recv, xs_send, xs_recv, zs_send, zs_recv,
):
    n = rn // 2
    half = n // 2
    row, z = lax.axis_index("row"), lax.axis_index("col")
    chip, core = row // 2, row % 2
    height, w = c_ref.shape
    ch = height // CHUNKS
    hb = out_ref.shape[0]

    def pos_of(p):
        return jnp.where(p % 2 == 0, p // 2, n - 1 - p // 2)

    def chip_at(pos):
        return jnp.where(pos < half, 2 * pos, 2 * (n - 1 - pos) + 1)

    def dev(p, k, zz):
        return (2 * p + k, zz)

    pos = pos_of(chip)
    step = 1 - 2 * core
    dist = ((pos - pos_of(z)) * step + n) % n
    holder = dist == 0
    ahead = dev(chip_at((pos + step + n) % n), core, z)
    sibling = dev(chip, 1 - core, z)

    def remote(src, dst, ss, rs, target):
        return pltpu.make_async_remote_copy(
            src_ref=src, dst_ref=dst, send_sem=ss, recv_sem=rs,
            device_id=target, device_id_type=pl.DeviceIdType.MESH,
        )

    def part(q):
        return pl.ds(pl.multiple_of(q * ch, ch), ch)

    def s_copy(q):
        return pltpu.make_async_copy(s_hbm.at[part(q)], s_buf.at[part(q)], s_sem.at[q])

    def up_copy(s, q):
        ref = rows.at[s, part(q)]
        return remote(ref, ref, up_send.at[s, q], z_recv.at[s, q], (row, jnp.minimum(z + 1, zn - 1)))

    def dn_copy(s, q):
        ref = rows.at[s, part(q)]
        return remote(ref, ref, dn_send.at[s, q], z_recv.at[s, q], (row, jnp.maximum(z - 1, 0)))

    def ring_copy(s, q, src):
        return remote(src.at[part(q)], cols.at[s, core, part(q)], ring_send.at[s, q], ring_recv.at[s, q], ahead)

    def sib_copy(s, q, src):
        return remote(src.at[part(q)], cols.at[s, core, part(q)], sib_send.at[s, q], sib_recv.at[s, q], sibling)

    def loc_copy(s, q):
        return pltpu.make_async_copy(rows.at[s, part(q)], cols.at[s, core, part(q)], loc_sem.at[s, q])

    for q in range(CHUNKS):
        s_copy(q).start()

    barrier = pltpu.get_barrier_semaphore()
    for d in range(1, n):
        pl.semaphore_signal(barrier, inc=1, device_id=dev((chip + d) % n, core, z), device_id_type=pl.DeviceIdType.MESH)
    for d in range(1, zn):
        pl.semaphore_signal(barrier, inc=1, device_id=(row, (z + d) % zn), device_id_type=pl.DeviceIdType.MESH)
    pl.semaphore_signal(barrier, inc=1, device_id=sibling, device_id_type=pl.DeviceIdType.MESH)

    def mask_c(i, carry):
        at = pl.ds(pl.multiple_of(i * BLK, BLK), BLK)
        for j in range(w // BLK):
            m = jnp.full((BLK, BLK), cmask[i, j].astype(F32), F32).astype(BF)
            rows[z, at, j * BLK:(j + 1) * BLK] = c_ref[at, j * BLK:(j + 1) * BLK] * m
        return carry

    lax.fori_loop(0, height // BLK, mask_c, 0)
    pl.semaphore_wait(barrier, n - 1 + zn - 1 + 1)

    def mask_s(i, carry):
        at = pl.ds(pl.multiple_of(i * BLK, BLK), BLK)
        for j in range(s_buf.shape[1] // BLK):
            m = jnp.full((BLK, BLK), smask[i, j].astype(F32), F32).astype(BF)
            s_buf[at, j * BLK:(j + 1) * BLK] = s_buf[at, j * BLK:(j + 1) * BLK] * m
        return carry

    def arrive(s, q, t, side):
        ok = jnp.logical_and(s >= 0, s < zn)
        if side:
            ok = jnp.logical_and(ok, t > 0)

        @pl.when(ok)
        def _():
            @pl.when(t > 0)
            def _():
                up_copy(s, q).wait_recv()

            if side == 0:
                @pl.when(z < zn - 1)
                def _():
                    up_copy(s, q).start()

            @pl.when(jnp.logical_and(z > 0, (t == 0) if side == 0 else True))
            def _():
                dn_copy(s, q).start()

            @pl.when(holder)
            def _():
                ring_copy(s, q, rows.at[s]).start()
                sib_copy(s, q, rows.at[s]).start()
                loc_copy(s, q).start()

    def relay(s, q, t, side):
        ok = jnp.logical_and(s >= 0, s < zn)
        if side:
            ok = jnp.logical_and(ok, t > 0)

        @pl.when(ok)
        def _():
            rows_t[s, :, part(q)] = rows[s, part(q)].T

            @pl.when(jnp.logical_not(holder))
            def _():
                src = cols.at[s, core]
                ring_copy(s, q, src).wait_recv()

                @pl.when(dist < n - 1)
                def _():
                    ring_copy(s, q, src).start()

                sib_copy(s, q, src).start()

    def multiply(s, q, t, side):
        ok = jnp.logical_and(s >= 0, s < zn)
        ok = jnp.logical_and(ok, t > (1 if side else 0))

        @pl.when(ok)
        def _():
            @pl.when(q == 0)
            def _():
                def settle(qq, carry):
                    @pl.when(holder)
                    def _():
                        loc_copy(s, qq).wait()

                    sib_copy(s, qq, cols.at[s, core]).wait_recv()
                    return carry

                lax.fori_loop(0, CHUNKS, settle, 0)

            total = jnp.dot(s_buf[part(q), :height], cols[s, 0], preferred_element_type=F32)
            total += jnp.dot(s_buf[part(q), height:], cols[s, 1], preferred_element_type=F32)
            prod[s, part(q)] = total.astype(BF)

    def tick(i, carry):
        t, q = i // CHUNKS, i % CHUNKS

        @pl.when(t < zn)
        def _():
            arrive(z - t, q, t, 0)
            arrive(z + t, q, t, 1)

        @pl.when(t == 0)
        def _():
            s_copy(q).wait()
            lax.fori_loop(q * (ch // BLK), (q + 1) * (ch // BLK), mask_s, 0)

        @pl.when(t < zn)
        def _():
            relay(z - t, q, t, 0)
            relay(z + t, q, t, 1)

        multiply(z - t + 1, q, t, 0)
        multiply(z + t - 1, q, t, 1)
        return carry

    lax.fori_loop(0, (zn + 1) * CHUNKS, tick, 0)

    def gs_copy(c):
        return remote(g_sib.at[c], g_got.at[c], gs_send.at[c], gs_recv.at[c], sibling)

    def contract(i, carry):
        c = (z + 1 + i) % zn

        def rowblock(s, carry):
            got = jnp.dot(rows_t[s], prod[c], preferred_element_type=F32)
            per = w // hb
            for b in range(per // 2):
                lo = got[2 * b * hb:(2 * b + 1) * hb]
                hi = got[(2 * b + 1) * hb:(2 * b + 2) * hb]
                g_own[c, s * (per // 2) + b] = jnp.where(core == 0, lo, hi)
                g_sib[c, s * (per // 2) + b] = jnp.where(core == 0, hi, lo)
            return carry

        lax.fori_loop(0, zn, rowblock, 0)
        gs_copy(c).start()
        return carry

    lax.fori_loop(0, zn, contract, 0)

    def xs_copy(c, d):
        target = (chip + d) % n
        return remote(x_out.at[c, target], x_in.at[c, d], xs_send.at[c, d], xs_recv.at[c, d], dev(target, core, z))

    def spread(i, carry):
        c = (z + 1 + i) % zn
        gs_copy(c).wait_recv()
        total = g_own[c] + g_got[c]
        g_own[c] = total
        x_out[c] = total.astype(BF)
        for d in range(1, n):
            xs_copy(c, d).start()
        return carry

    lax.fori_loop(0, zn, spread, 0)

    def zs_copy(d):
        return remote(z_out.at[d], z_in.at[d], zs_send.at[d], zs_recv.at[d], (row, (z + d) % zn))

    def plane_sum(c):
        total = g_own[c, chip]
        for d in range(1, n):
            xs_copy(c, d).wait_recv()
            total += x_in[c, d].astype(F32)
        return total

    def onward(d, carry):
        c = (z + d) % zn
        z_out[d] = plane_sum(c).astype(BF)
        zs_copy(d).start()
        return carry

    lax.fori_loop(1, zn, onward, 0)
    total = plane_sum(z)
    for d in range(1, zn):
        zs_copy(d).wait_recv()
        total += z_in[d].astype(F32)
    out_ref[...] = total

    def drain(i, carry):
        s, q = i // CHUNKS, i % CHUNKS

        @pl.when(jnp.logical_and(s <= z, z < zn - 1))
        def _():
            up_copy(s, q).wait_send()

        @pl.when(jnp.logical_and(s >= z, z > 0))
        def _():
            dn_copy(s, q).wait_send()

        @pl.when(dist < n - 1)
        def _():
            ring_copy(s, q, cols.at[s, core]).wait_send()

        sib_copy(s, q, cols.at[s, core]).wait_send()
        return carry

    lax.fori_loop(0, zn * CHUNKS, drain, 0)

    def drain_sums(c, carry):
        gs_copy(c).wait_send()
        for d in range(1, n):
            xs_copy(c, d).wait_send()
        return carry

    lax.fori_loop(0, zn, drain_sums, 0)
    for d in range(1, zn):
        zs_copy(d).wait_send()


def local(rn, zn, coeffs, intersection, coeff_mask, intersection_mask):
    height, w = coeffs.shape
    width = intersection.shape[1]
    n = rn // 2
    hb = zn * w // rn
    dma = pltpu.SemaphoreType.DMA
    flops = 2 * height * width * w * zn + 2 * height * (w * zn) ** 2
    return pl.pallas_call(
        functools.partial(kernel, rn, zn),
        out_shape=jax.ShapeDtypeStruct((hb, w), F32),
        in_specs=[
            pl.BlockSpec(memory_space=pltpu.SMEM),
            pl.BlockSpec(memory_space=pltpu.SMEM),
            pl.BlockSpec(memory_space=pltpu.VMEM),
            pl.BlockSpec(memory_space=pl.ANY),
        ],
        out_specs=pl.BlockSpec(memory_space=pltpu.VMEM),
        scratch_shapes=[
            pltpu.VMEM((height, width), BF),
            pltpu.VMEM((zn, height, w), BF),
            pltpu.VMEM((zn, w, height), BF),
            pltpu.VMEM((zn, 2, height, w), BF),
            pltpu.VMEM((zn, height, w), BF),
            pltpu.VMEM((zn, n, hb, w), F32),
            pltpu.VMEM((zn, n, hb, w), F32),
            pltpu.VMEM((zn, n, hb, w), F32),
            pltpu.VMEM((zn, n, hb, w), BF),
            pltpu.VMEM((zn, n, hb, w), BF),
            pltpu.VMEM((zn, hb, w), BF),
            pltpu.VMEM((zn, hb, w), BF),
            dma((CHUNKS,)),
        ] + [dma((zn, CHUNKS))] * 8 + [
            dma((zn,)), dma((zn,)),
            dma((zn, n)), dma((zn, n)),
            dma((zn,)), dma((zn,)),
        ],
        compiler_params=pltpu.CompilerParams(
            collective_id=0, has_side_effects=True, vmem_limit_bytes=60 * 1024 * 1024
        ),
        cost_estimate=pl.CostEstimate(flops=flops, bytes_accessed=2 * height * width, transcendentals=0),
    )(coeff_mask, intersection_mask, coeffs, intersection)


def solution(mesh):
    return jax.shard_map(
        functools.partial(local, mesh.shape["row"], mesh.shape["col"]),
        mesh=mesh,
        in_specs=(P("row", "col"), P("row", "col"), P("row", "col"), P("row", "col")),
        out_specs=P("row", "col"),
        check_vma=False,
    )
```

```python
import functools

import jax
import jax.numpy as jnp
from jax import lax
from jax.experimental import pallas as pl
from jax.experimental.pallas import tpu as pltpu
from jax.sharding import PartitionSpec as P

BLK = 128
CHUNKS = 8
PAIRS = CHUNKS // 2
BF = jnp.bfloat16
F32 = jnp.float32


def kernel(
    rn, zn, cmask, smask, c_ref, s_hbm, out_ref,
    s_buf, rows, rows_t, cols, prod, g_own, g_sib, g_got, x_out, x_in, z_out, z_in,
    s_sem, up_send, dn_send, z_recv, ring_send, ring_recv, sib_send, sib_recv, loc_sem,
    gs_send, gs_recv, xs_send, xs_recv, zs_send, zs_recv,
):
    n = rn // 2
    half = n // 2
    row, z = lax.axis_index("row"), lax.axis_index("col")
    chip, core = row // 2, row % 2
    height, w = c_ref.shape
    ch = height // CHUNKS
    hb = out_ref.shape[0]

    def pos_of(p):
        return jnp.where(p % 2 == 0, p // 2, n - 1 - p // 2)

    def chip_at(pos):
        return jnp.where(pos < half, 2 * pos, 2 * (n - 1 - pos) + 1)

    def dev(p, k, zz):
        return (2 * p + k, zz)

    pos = pos_of(chip)
    holder = chip == z

    def way(q):
        return 1 - 2 * (core)

    def dist(q):
        return ((pos - pos_of(z)) * way(q) + n) % n

    def ahead(q):
        return dev(chip_at((pos + way(q) + n) % n), core, z)

    sibling = dev(chip, 1 - core, z)

    def remote(src, dst, ss, rs, target):
        return pltpu.make_async_remote_copy(
            src_ref=src, dst_ref=dst, send_sem=ss, recv_sem=rs,
            device_id=target, device_id_type=pl.DeviceIdType.MESH,
        )

    def part(q):
        return pl.ds(pl.multiple_of(q * ch, ch), ch)

    def s_copy(q):
        return pltpu.make_async_copy(s_hbm.at[part(q)], s_buf.at[part(q)], s_sem.at[q])

    def up_copy(s, q):
        ref = rows.at[s, part(q)]
        return remote(ref, ref, up_send.at[s, q], z_recv.at[s, q], (row, jnp.minimum(z + 1, zn - 1)))

    def dn_copy(s, q):
        ref = rows.at[s, part(q)]
        return remote(ref, ref, dn_send.at[s, q], z_recv.at[s, q], (row, jnp.maximum(z - 1, 0)))

    def ring_copy(s, q, src):
        return remote(src.at[part(q)], cols.at[s, core, part(q)], ring_send.at[s, q], ring_recv.at[s, q], ahead(q))

    def sib_copy(s, q, src):
        return remote(src.at[part(q)], cols.at[s, core, part(q)], sib_send.at[s, q], sib_recv.at[s, q], sibling)

    def loc_copy(s, q):
        return pltpu.make_async_copy(rows.at[s, part(q)], cols.at[s, core, part(q)], loc_sem.at[s, q])

    for q in range(CHUNKS):
        s_copy(q).start()

    barrier = pltpu.get_barrier_semaphore()
    for d in range(1, n):
        pl.semaphore_signal(barrier, inc=1, device_id=dev((chip + d) % n, core, z), device_id_type=pl.DeviceIdType.MESH)
    for d in range(1, zn):
        pl.semaphore_signal(barrier, inc=1, device_id=(row, (z + d) % zn), device_id_type=pl.DeviceIdType.MESH)
    pl.semaphore_signal(barrier, inc=1, device_id=sibling, device_id_type=pl.DeviceIdType.MESH)

    def mask_c(i, carry):
        at = pl.ds(pl.multiple_of(i * BLK, BLK), BLK)
        for j in range(w // BLK):
            m = jnp.full((BLK, BLK), cmask[i, j].astype(F32), F32).astype(BF)
            rows[z, at, j * BLK:(j + 1) * BLK] = c_ref[at, j * BLK:(j + 1) * BLK] * m
        return carry

    lax.fori_loop(0, height // BLK, mask_c, 0)
    pl.semaphore_wait(barrier, n - 1 + zn - 1 + 1)

    def mask_s(i, carry):
        at = pl.ds(pl.multiple_of(i * BLK, BLK), BLK)
        for j in range(s_buf.shape[1] // BLK):
            m = jnp.full((BLK, BLK), smask[i, j].astype(F32), F32).astype(BF)
            s_buf[at, j * BLK:(j + 1) * BLK] = s_buf[at, j * BLK:(j + 1) * BLK] * m
        return carry

    def arrive(s, q, t, side):
        ok = jnp.logical_and(s >= 0, s < zn)
        if side:
            ok = jnp.logical_and(ok, t > 0)

        @pl.when(ok)
        def _():
            @pl.when(t > 0)
            def _():
                up_copy(s, q).wait_recv()

            if side == 0:
                @pl.when(z < zn - 1)
                def _():
                    up_copy(s, q).start()

            @pl.when(jnp.logical_and(z > 0, (t == 0) if side == 0 else True))
            def _():
                dn_copy(s, q).start()

            @pl.when(holder)
            def _():
                ring_copy(s, q, rows.at[s]).start()
                sib_copy(s, q, rows.at[s]).start()
                loc_copy(s, q).start()

    def relay(s, q, t, side):
        ok = jnp.logical_and(s >= 0, s < zn)
        if side:
            ok = jnp.logical_and(ok, t > 0)

        @pl.when(ok)
        def _():
            rows_t[s, :, part(q)] = rows[s, part(q)].T

            @pl.when(jnp.logical_not(holder))
            def _():
                src = cols.at[s, core]
                ring_copy(s, q, src).wait_recv()

                @pl.when(dist(q) < n - 1)
                def _():
                    ring_copy(s, q, src).start()

                sib_copy(s, q, src).start()

    def multiply(s, q, t, side):
        ok = jnp.logical_and(s >= 0, s < zn)
        ok = jnp.logical_and(ok, t > (1 if side else 0))

        @pl.when(ok)
        def _():
            @pl.when(q == 0)
            def _():
                def settle(qq, carry):
                    @pl.when(holder)
                    def _():
                        loc_copy(s, qq).wait()

                    sib_copy(s, qq, cols.at[s, core]).wait_recv()
                    return carry

                lax.fori_loop(0, CHUNKS, settle, 0)

            at = pl.ds(pl.multiple_of(q * 2 * ch, 2 * ch), 2 * ch)
            total = jnp.dot(s_buf[at, :height], cols[s, 0], preferred_element_type=F32)
            total += jnp.dot(s_buf[at, height:], cols[s, 1], preferred_element_type=F32)
            prod[s, at] = total.astype(BF)

    def tick(i, carry):
        t = i // PAIRS
        first = 2 * (i % PAIRS)

        @pl.when(t < zn)
        def _():
            for q in (first, first + 1):
                arrive(z - t, q, t, 0)
                arrive(z + t, q, t, 1)

        @pl.when(t == 0)
        def _():
            for q in (first, first + 1):
                s_copy(q).wait()
            lax.fori_loop(first * (ch // BLK), (first + 2) * (ch // BLK), mask_s, 0)

        for parity in range(2):
            late = i - dist(parity)

            @pl.when(jnp.logical_and(late >= 0, late < zn * PAIRS))
            def _():
                t, q = late // PAIRS, 2 * (late % PAIRS) + parity
                relay(z - t, q, t, 0)
                relay(z + t, q, t, 1)

        late = i - (n - 1)

        @pl.when(late >= PAIRS)
        def _():
            t, q = late // PAIRS, late % PAIRS
            multiply(z - t + 1, q, t, 0)
            multiply(z + t - 1, q, t, 1)

        return carry

    lax.fori_loop(0, (zn + 1) * PAIRS + n - 1, tick, 0)

    def gs_copy(c):
        return remote(g_sib.at[c], g_got.at[c], gs_send.at[c], gs_recv.at[c], sibling)

    def contract(i):
        c = (z + 1 + i) % zn

        def rowblock(s, carry):
            got = jnp.dot(rows_t[s], prod[c], preferred_element_type=F32)
            per = w // hb
            for b in range(per // 2):
                lo = got[2 * b * hb:(2 * b + 1) * hb]
                hi = got[(2 * b + 1) * hb:(2 * b + 2) * hb]
                g_own[c, s * (per // 2) + b] = jnp.where(core == 0, lo, hi)
                g_sib[c, s * (per // 2) + b] = jnp.where(core == 0, hi, lo)
            return carry

        lax.fori_loop(0, zn, rowblock, 0)
        gs_copy(c).start()

    def xs_copy(c, d):
        target = (chip + d) % n
        return remote(x_out.at[c, target], x_in.at[c, d], xs_send.at[c, d], xs_recv.at[c, d], dev(target, core, z))

    def spread(i):
        c = (z + 1 + i) % zn
        gs_copy(c).wait_recv()
        total = g_own[c] + g_got[c]
        g_own[c] = total
        x_out[c] = total.astype(BF)
        for d in range(1, n):
            xs_copy(c, d).start()

    def stage(i, carry):
        @pl.when(i < zn)
        def _():
            contract(i)

        @pl.when(i > 0)
        def _():
            spread(i - 1)

        return carry

    lax.fori_loop(0, zn + 1, stage, 0)

    def zs_copy(d):
        return remote(z_out.at[d], z_in.at[d], zs_send.at[d], zs_recv.at[d], (row, (z + d) % zn))

    def plane_sum(c):
        total = g_own[c, chip]
        for d in range(1, n):
            xs_copy(c, d).wait_recv()
            total += x_in[c, d].astype(F32)
        return total

    def onward(d, carry):
        c = (z + d) % zn
        z_out[d] = plane_sum(c).astype(BF)
        zs_copy(d).start()
        return carry

    lax.fori_loop(1, zn, onward, 0)
    total = plane_sum(z)
    for d in range(1, zn):
        zs_copy(d).wait_recv()
        total += z_in[d].astype(F32)
    out_ref[...] = total

    def drain(i, carry):
        s, q = i // CHUNKS, i % CHUNKS

        @pl.when(jnp.logical_and(s <= z, z < zn - 1))
        def _():
            up_copy(s, q).wait_send()

        @pl.when(jnp.logical_and(s >= z, z > 0))
        def _():
            dn_copy(s, q).wait_send()

        @pl.when(dist(q) < n - 1)
        def _():
            ring_copy(s, q, cols.at[s, core]).wait_send()

        sib_copy(s, q, cols.at[s, core]).wait_send()
        return carry

    lax.fori_loop(0, zn * CHUNKS, drain, 0)

    def drain_sums(c, carry):
        gs_copy(c).wait_send()
        for d in range(1, n):
            xs_copy(c, d).wait_send()
        return carry

    lax.fori_loop(0, zn, drain_sums, 0)
    for d in range(1, zn):
        zs_copy(d).wait_send()


def local(rn, zn, coeffs, intersection, coeff_mask, intersection_mask):
    height, w = coeffs.shape
    width = intersection.shape[1]
    n = rn // 2
    hb = zn * w // rn
    dma = pltpu.SemaphoreType.DMA
    flops = 2 * height * width * w * zn + 2 * height * (w * zn) ** 2
    return pl.pallas_call(
        functools.partial(kernel, rn, zn),
        out_shape=jax.ShapeDtypeStruct((hb, w), F32),
        in_specs=[
            pl.BlockSpec(memory_space=pltpu.SMEM),
            pl.BlockSpec(memory_space=pltpu.SMEM),
            pl.BlockSpec(memory_space=pltpu.VMEM),
            pl.BlockSpec(memory_space=pl.ANY),
        ],
        out_specs=pl.BlockSpec(memory_space=pltpu.VMEM),
        scratch_shapes=[
            pltpu.VMEM((height, width), BF),
            pltpu.VMEM((zn, height, w), BF),
            pltpu.VMEM((zn, w, height), BF),
            pltpu.VMEM((zn, 2, height, w), BF),
            pltpu.VMEM((zn, height, w), BF),
            pltpu.VMEM((zn, n, hb, w), F32),
            pltpu.VMEM((zn, n, hb, w), F32),
            pltpu.VMEM((zn, n, hb, w), F32),
            pltpu.VMEM((zn, n, hb, w), BF),
            pltpu.VMEM((zn, n, hb, w), BF),
            pltpu.VMEM((zn, hb, w), BF),
            pltpu.VMEM((zn, hb, w), BF),
            dma((CHUNKS,)),
        ] + [dma((zn, CHUNKS))] * 8 + [
            dma((zn,)), dma((zn,)),
            dma((zn, n)), dma((zn, n)),
            dma((zn,)), dma((zn,)),
        ],
        compiler_params=pltpu.CompilerParams(
            collective_id=0, has_side_effects=True, vmem_limit_bytes=60 * 1024 * 1024
        ),
        cost_estimate=pl.CostEstimate(flops=flops, bytes_accessed=2 * height * width, transcendentals=0),
    )(coeff_mask, intersection_mask, coeffs, intersection)


def solution(mesh):
    return jax.shard_map(
        functools.partial(local, mesh.shape["row"], mesh.shape["col"]),
        mesh=mesh,
        in_specs=(P("row", "col"), P("row", "col"), P("row", "col"), P("row", "col")),
        out_specs=P("row", "col"),
        check_vma=False,
    )
```

```python
import functools

import jax
import jax.numpy as jnp
from jax import lax
from jax.experimental import pallas as pl
from jax.experimental.pallas import tpu as pltpu
from jax.sharding import PartitionSpec as P

BLK = 128
CHUNKS = 8
PAIRS = CHUNKS // 2
BF = jnp.bfloat16
F32 = jnp.float32


def kernel(
    rn, zn, cmask, smask, c_ref, s_hbm, out_ref,
    s_buf, rows, rows_t, cols, prod, g_own, g_sib, g_got, x_out, x_in, z_out, z_in,
    s_sem, up_send, dn_send, z_recv, ring_send, ring_recv, sib_send, sib_recv, loc_sem,
    gs_send, gs_recv, xs_send, xs_recv, zs_send, zs_recv,
):
    n = rn // 2
    half = n // 2
    row, z = lax.axis_index("row"), lax.axis_index("col")
    chip, core = row // 2, row % 2
    height, w = c_ref.shape
    ch = height // CHUNKS
    hb = out_ref.shape[0]

    def pos_of(p):
        return jnp.where(p % 2 == 0, p // 2, n - 1 - p // 2)

    def chip_at(pos):
        return jnp.where(pos < half, 2 * pos, 2 * (n - 1 - pos) + 1)

    def dev(p, k, zz):
        return (2 * p + k, zz)

    pos = pos_of(chip)
    holder = chip == z

    def way(q):
        return 1 - 2 * (core)

    def dist(q):
        return ((pos - pos_of(z)) * way(q) + n) % n

    def ahead(q):
        return dev(chip_at((pos + way(q) + n) % n), core, z)

    sibling = dev(chip, 1 - core, z)

    def remote(src, dst, ss, rs, target):
        return pltpu.make_async_remote_copy(
            src_ref=src, dst_ref=dst, send_sem=ss, recv_sem=rs,
            device_id=target, device_id_type=pl.DeviceIdType.MESH,
        )

    def part(q):
        return pl.ds(pl.multiple_of(q * ch, ch), ch)

    def s_copy(q):
        return pltpu.make_async_copy(s_hbm.at[part(q)], s_buf.at[part(q)], s_sem.at[q])

    def up_copy(s, q):
        ref = rows.at[s, part(q)]
        return remote(ref, ref, up_send.at[s, q], z_recv.at[s, q], (row, jnp.minimum(z + 1, zn - 1)))

    def dn_copy(s, q):
        ref = rows.at[s, part(q)]
        return remote(ref, ref, dn_send.at[s, q], z_recv.at[s, q], (row, jnp.maximum(z - 1, 0)))

    def ring_copy(s, q, src):
        return remote(src.at[part(q)], cols.at[s, core, part(q)], ring_send.at[s, q], ring_recv.at[s, q], ahead(q))

    def sib_copy(s, q, src):
        return remote(src.at[part(q)], cols.at[s, core, part(q)], sib_send.at[s, q], sib_recv.at[s, q], sibling)

    def loc_copy(s, q):
        return pltpu.make_async_copy(rows.at[s, part(q)], cols.at[s, core, part(q)], loc_sem.at[s, q])

    for q in range(CHUNKS):
        s_copy(q).start()

    barrier = pltpu.get_barrier_semaphore()
    for d in range(1, n):
        pl.semaphore_signal(barrier, inc=1, device_id=dev((chip + d) % n, core, z), device_id_type=pl.DeviceIdType.MESH)
    for d in range(1, zn):
        pl.semaphore_signal(barrier, inc=1, device_id=(row, (z + d) % zn), device_id_type=pl.DeviceIdType.MESH)
    pl.semaphore_signal(barrier, inc=1, device_id=sibling, device_id_type=pl.DeviceIdType.MESH)

    def mask_c(i, carry):
        at = pl.ds(pl.multiple_of(i * BLK, BLK), BLK)
        for j in range(w // BLK):
            m = jnp.full((BLK, BLK), cmask[i, j].astype(F32), F32).astype(BF)
            rows[z, at, j * BLK:(j + 1) * BLK] = c_ref[at, j * BLK:(j + 1) * BLK] * m
        return carry

    lax.fori_loop(0, height // BLK, mask_c, 0)
    pl.semaphore_wait(barrier, n - 1 + zn - 1 + 1)

    def mask_s(i, carry):
        at = pl.ds(pl.multiple_of(i * BLK, BLK), BLK)
        for j in range(s_buf.shape[1] // BLK):
            m = jnp.full((BLK, BLK), smask[i, j].astype(F32), F32).astype(BF)
            s_buf[at, j * BLK:(j + 1) * BLK] = s_buf[at, j * BLK:(j + 1) * BLK] * m
        return carry

    def arrive(s, q, t, side):
        ok = jnp.logical_and(s >= 0, s < zn)
        if side:
            ok = jnp.logical_and(ok, t > 0)

        @pl.when(ok)
        def _():
            @pl.when(t > 0)
            def _():
                up_copy(s, q).wait_recv()

            if side == 0:
                @pl.when(z < zn - 1)
                def _():
                    up_copy(s, q).start()

            @pl.when(jnp.logical_and(z > 0, (t == 0) if side == 0 else True))
            def _():
                dn_copy(s, q).start()

            @pl.when(holder)
            def _():
                ring_copy(s, q, rows.at[s]).start()
                sib_copy(s, q, rows.at[s]).start()
                loc_copy(s, q).start()

    def relay(s, q, t, side):
        ok = jnp.logical_and(s >= 0, s < zn)
        if side:
            ok = jnp.logical_and(ok, t > 0)

        @pl.when(ok)
        def _():
            @pl.when(jnp.logical_not(holder))
            def _():
                src = cols.at[s, core]
                ring_copy(s, q, src).wait_recv()

                @pl.when(dist(q) < n - 1)
                def _():
                    ring_copy(s, q, src).start()

                sib_copy(s, q, src).start()

            rows_t[s, :, part(q)] = rows[s, part(q)].T

    def multiply(s, q, t, side):
        ok = jnp.logical_and(s >= 0, s < zn)
        ok = jnp.logical_and(ok, t > (1 if side else 0))

        @pl.when(ok)
        def _():
            @pl.when(q == 0)
            def _():
                def settle(qq, carry):
                    @pl.when(holder)
                    def _():
                        loc_copy(s, qq).wait()

                    sib_copy(s, qq, cols.at[s, core]).wait_recv()
                    return carry

                lax.fori_loop(0, CHUNKS, settle, 0)

            at = pl.ds(pl.multiple_of(q * 2 * ch, 2 * ch), 2 * ch)
            total = jnp.dot(s_buf[at, :height], cols[s, 0], preferred_element_type=F32)
            total += jnp.dot(s_buf[at, height:], cols[s, 1], preferred_element_type=F32)
            prod[s, at] = total.astype(BF)

    def tick(i, carry):
        t = i // PAIRS
        first = 2 * (i % PAIRS)

        @pl.when(t < zn)
        def _():
            for q in (first, first + 1):
                arrive(z - t, q, t, 0)
                arrive(z + t, q, t, 1)

        @pl.when(t == 0)
        def _():
            for q in (first, first + 1):
                s_copy(q).wait()
            lax.fori_loop(first * (ch // BLK), (first + 2) * (ch // BLK), mask_s, 0)

        for parity in range(2):
            late = i - dist(parity)

            @pl.when(jnp.logical_and(late >= 0, late < zn * PAIRS))
            def _():
                t, q = late // PAIRS, 2 * (late % PAIRS) + parity
                relay(z - t, q, t, 0)
                relay(z + t, q, t, 1)

        late = i - (n - 1)

        @pl.when(late >= PAIRS)
        def _():
            t, q = late // PAIRS, late % PAIRS
            multiply(z - t + 1, q, t, 0)
            multiply(z + t - 1, q, t, 1)

        return carry

    lax.fori_loop(0, (zn + 1) * PAIRS + n - 1, tick, 0)

    def gs_copy(c):
        return remote(g_sib.at[c], g_got.at[c], gs_send.at[c], gs_recv.at[c], sibling)

    def contract(i):
        c = (z + 1 + i) % zn

        def rowblock(s, carry):
            got = jnp.dot(rows_t[s], prod[c], preferred_element_type=F32)
            per = w // hb
            for b in range(per // 2):
                lo = got[2 * b * hb:(2 * b + 1) * hb]
                hi = got[(2 * b + 1) * hb:(2 * b + 2) * hb]
                g_own[c, s * (per // 2) + b] = jnp.where(core == 0, lo, hi)
                g_sib[c, s * (per // 2) + b] = jnp.where(core == 0, hi, lo)
            return carry

        lax.fori_loop(0, zn, rowblock, 0)
        gs_copy(c).start()

    def xs_copy(c, d):
        target = (chip + d) % n
        return remote(x_out.at[c, target], x_in.at[c, d], xs_send.at[c, d], xs_recv.at[c, d], dev(target, core, z))

    def spread(i):
        c = (z + 1 + i) % zn
        gs_copy(c).wait_recv()
        total = g_own[c] + g_got[c]
        g_own[c] = total
        x_out[c] = total.astype(BF)
        for d in range(1, n):
            xs_copy(c, d).start()

    def stage(i, carry):
        @pl.when(i < zn)
        def _():
            contract(i)

        @pl.when(i > 0)
        def _():
            spread(i - 1)

        return carry

    lax.fori_loop(0, zn + 1, stage, 0)

    def zs_copy(d):
        return remote(z_out.at[d], z_in.at[d], zs_send.at[d], zs_recv.at[d], (row, (z + d) % zn))

    def plane_sum(c):
        total = g_own[c, chip]
        for d in range(1, n):
            xs_copy(c, d).wait_recv()
            total += x_in[c, d].astype(F32)
        return total

    def onward(d, carry):
        c = (z + d) % zn
        z_out[d] = plane_sum(c).astype(BF)
        zs_copy(d).start()
        return carry

    lax.fori_loop(1, zn, onward, 0)
    total = plane_sum(z)
    for d in range(1, zn):
        zs_copy(d).wait_recv()
        total += z_in[d].astype(F32)
    out_ref[...] = total

    def drain(i, carry):
        s, q = i // CHUNKS, i % CHUNKS

        @pl.when(jnp.logical_and(s <= z, z < zn - 1))
        def _():
            up_copy(s, q).wait_send()

        @pl.when(jnp.logical_and(s >= z, z > 0))
        def _():
            dn_copy(s, q).wait_send()

        @pl.when(dist(q) < n - 1)
        def _():
            ring_copy(s, q, cols.at[s, core]).wait_send()

        sib_copy(s, q, cols.at[s, core]).wait_send()
        return carry

    lax.fori_loop(0, zn * CHUNKS, drain, 0)

    def drain_sums(c, carry):
        gs_copy(c).wait_send()
        for d in range(1, n):
            xs_copy(c, d).wait_send()
        return carry

    lax.fori_loop(0, zn, drain_sums, 0)
    for d in range(1, zn):
        zs_copy(d).wait_send()


def local(rn, zn, coeffs, intersection, coeff_mask, intersection_mask):
    height, w = coeffs.shape
    width = intersection.shape[1]
    n = rn // 2
    hb = zn * w // rn
    dma = pltpu.SemaphoreType.DMA
    flops = 2 * height * width * w * zn + 2 * height * (w * zn) ** 2
    return pl.pallas_call(
        functools.partial(kernel, rn, zn),
        out_shape=jax.ShapeDtypeStruct((hb, w), F32),
        in_specs=[
            pl.BlockSpec(memory_space=pltpu.SMEM),
            pl.BlockSpec(memory_space=pltpu.SMEM),
            pl.BlockSpec(memory_space=pltpu.VMEM),
            pl.BlockSpec(memory_space=pl.ANY),
        ],
        out_specs=pl.BlockSpec(memory_space=pltpu.VMEM),
        scratch_shapes=[
            pltpu.VMEM((height, width), BF),
            pltpu.VMEM((zn, height, w), BF),
            pltpu.VMEM((zn, w, height), BF),
            pltpu.VMEM((zn, 2, height, w), BF),
            pltpu.VMEM((zn, height, w), BF),
            pltpu.VMEM((zn, n, hb, w), F32),
            pltpu.VMEM((zn, n, hb, w), F32),
            pltpu.VMEM((zn, n, hb, w), F32),
            pltpu.VMEM((zn, n, hb, w), BF),
            pltpu.VMEM((zn, n, hb, w), BF),
            pltpu.VMEM((zn, hb, w), BF),
            pltpu.VMEM((zn, hb, w), BF),
            dma((CHUNKS,)),
        ] + [dma((zn, CHUNKS))] * 8 + [
            dma((zn,)), dma((zn,)),
            dma((zn, n)), dma((zn, n)),
            dma((zn,)), dma((zn,)),
        ],
        compiler_params=pltpu.CompilerParams(
            collective_id=0, has_side_effects=True, vmem_limit_bytes=60 * 1024 * 1024
        ),
        cost_estimate=pl.CostEstimate(flops=flops, bytes_accessed=2 * height * width, transcendentals=0),
    )(coeff_mask, intersection_mask, coeffs, intersection)


def solution(mesh):
    return jax.shard_map(
        functools.partial(local, mesh.shape["row"], mesh.shape["col"]),
        mesh=mesh,
        in_specs=(P("row", "col"), P("row", "col"), P("row", "col"), P("row", "col")),
        out_specs=P("row", "col"),
        check_vma=False,
    )
```
